512 devices in a mesh: dp: 32 (over y, x, core), mp: 16 (over z).
Axes of the slice: x: 4, y: 4, z: 16, core: 2. Of those that a mesh axis runs over, the one named last changes fastest.
Arguments:
- replica_grads: bfloat16 [32, 4096, 2048], P('dp', None, 'mp'), may hold values from -64 to 64, as said below
- weights: float32 [4096, 2048], P('dp', 'mp'), may hold values from -0.00390625 to 0.00390625
- row_state: float32 [4096], P('dp'), may hold values from 0.02 to 0.5
- col_state: float32 [2048], P('mp'), may hold values from 0.02 to 0.5
Outputs:
- new_weights: float32 [4096, 2048], P(None, 'mp')
- update: float32 [4096, 2048], P('dp', 'mp')
- new_row_state: float32 [4096], P('dp')
- new_col_state: float32 [2048], P('mp')
- rms_value: float32 [], replicated
The draws below stay inside these ranges and needn't reach their ends.
Inputs may be any that keep to these rules, and one draw needn't show every extreme that they name: `replica_grads`: gradient entries have row and column scales that differ over the matrix.
All inputs are finite; a program needn't handle non-finite values.
Results may differ from the reference program's by a relative error of at most 0.0003.
Values sent between devices are 32-bit elements; how exact they have to be, the bound alone decides.
No kernel may reach another device: no remote copies, remote signals or barrier semaphores. Data moves between devices by JAX's collectives and lax.ppermute only.
A program may use at most 64 MiB of HBM per device.

```python
import math
import jax
import jax.numpy as jnp
from jax import lax

D = 4096
STEP = 10
FLAT = 2048
REPLICAS = 32


def draw_replica_grads(key, part):
    key = jax.random.fold_in(key, 3)
    key_rows, key_cols, key_noise = jax.random.split(key, 3)
    rise_rows = jnp.exp(math.log(3.0) * jnp.arange(D, dtype=jnp.float32) / D)
    rise_cols = jnp.exp(math.log(3.0) * jnp.arange(FLAT, dtype=jnp.float32) / FLAT)
    row_scale = jnp.exp(jax.random.uniform(key_rows, (D,), jnp.float32) * math.log(10.0)) * rise_rows / 8.8
    col_scale = jnp.exp(jax.random.uniform(key_cols, (FLAT,), jnp.float32) * math.log(10.0)) * rise_cols / 8.8
    noise = jnp.clip(jax.random.normal(key_noise, (REPLICAS, D, FLAT), jnp.float32), -4.0, 4.0)
    values = noise * row_scale[None, :, None] * col_scale[None, None, :] * math.sqrt(REPLICAS)
    return jnp.clip(values, -64.0, 64.0).astype(jnp.bfloat16)


def levels(stream_key, shape, cuts, low, largest):
    def one(axis_at, parts):
        steps = jax.random.uniform(jax.random.fold_in(jax.random.fold_in(stream_key, 6), axis_at), (parts,), jnp.float32, low / len(cuts), largest / len(cuts))
        return jnp.repeat(jnp.exp(steps), shape[axis_at] // parts).reshape((-1,) + (1,) * (len(shape) - axis_at - 1))

    gain = one(*cuts[0])
    for cut in cuts[1:]:
        gain = gain * one(*cut)
    return gain


def bell_draw(key, extent, width, most, shards=(), held_as=jnp.bfloat16):
    array = width * jax.random.normal(key, extent, jnp.float32)
    if shards:
        array = array * levels(key, extent, shards, -0.22, 0.18)
    return jnp.clip(array, -most, most).astype(held_as)


def setup_inputs(seed: int = 0) -> dict:
    splits = jax.random.split(jax.random.key(seed), 5)
    replica_grads = draw_replica_grads(jax.random.fold_in(splits[4], 71), 0)
    weights = bell_draw(splits[1], (D, FLAT), 0.0003, 0.00390625, ((0, 32), (1, 16)), jnp.float32)
    row_state = jnp.clip(jnp.exp(math.log(0.5) - 3.218876 * jax.random.uniform(splits[2], (D,), jnp.float32) ** levels(splits[2], (D,), ((0, 32),), -0.2, 0.2)), 0.02, 0.5)
    col_state = jnp.clip(jnp.exp(math.log(0.5) - 3.218876 * jax.random.uniform(splits[3], (FLAT,), jnp.float32) ** levels(splits[3], (FLAT,), ((0, 16),), -0.2, 0.2)), 0.02, 0.5)
    return {"replica_grads": replica_grads, "weights": weights, "row_state": row_state, "col_state": col_state}


def reference(replica_grads, weights, row_state, col_state):
    decay_rate = 1.0 - float(STEP) ** (-0.8)

    def accumulate(position, running):
        return running + replica_grads[position].astype(jnp.float32)
    summed = lax.fori_loop(0, REPLICAS, accumulate, jnp.zeros((D, FLAT), jnp.float32))
    mean_grad = summed / REPLICAS
    square = mean_grad * mean_grad + 1e-30
    row_new = decay_rate * row_state + (1.0 - decay_rate) * (lax.optimization_barrier(jnp.sum(square, 1)) / FLAT)
    col_new = decay_rate * col_state + (1.0 - decay_rate) * (lax.optimization_barrier(jnp.sum(square, 0)) / D)
    row_mean = jnp.sum(row_new) / D
    raw_update = mean_grad / jnp.sqrt(row_new[:, None] * col_new[None, :] / row_mean)
    rms_value = jnp.sqrt(jnp.sum(raw_update * raw_update) / (D * FLAT))
    update = raw_update / jnp.maximum(1.0, rms_value)
    new_weights = weights - 0.001 * update
    return (new_weights, update, row_new, col_new, rms_value)
```

```python
import jax
import jax.numpy as jnp
from jax import lax
from jax.sharding import Mesh, PartitionSpec as P

D = 4096
STEP = 10
FLAT = 2048
Q, C, Z = 16, 2, 16
DP = ("q", "c")
SWAP = [(0, 1), (1, 0)]


def share(x, axes, n):
    return lax.all_to_all(
        jnp.broadcast_to(x[None], (n, *x.shape)), axes, 0, 0, tiled=True
    )


def per_device(replica_grads, weights, row_state, col_state):
    decay_rate = 1.0 - float(STEP) ** (-0.8)
    rows = D // (Q * C)
    cols = weights.shape[1]
    core = lax.axis_index("c")

    grads = replica_grads[0].reshape(Q, C, rows, cols)
    kept = lax.dynamic_index_in_dim(grads, core, 1, False).astype(jnp.float32)
    sent = lax.dynamic_index_in_dim(grads, 1 - core, 1, False).astype(jnp.float32)
    chip = kept + lax.ppermute(sent, "c", SWAP)
    mean_grad = jnp.sum(lax.all_to_all(chip, "q", 0, 0, tiled=True), 0) / (Q * C)

    square = mean_grad * mean_grad + 1e-30
    col_sums = jnp.sum(share(jnp.sum(square, 0)[None], DP, Q * C), (0, 1))
    col_new = decay_rate * col_state + (1.0 - decay_rate) * (col_sums / D)
    col_inv = 1.0 / col_new
    both = jnp.stack([jnp.sum(square, 1), jnp.sum(mean_grad * mean_grad * col_inv, 1)])
    both = jnp.sum(share(both, "z", Z), 0)
    row_new = decay_rate * row_state + (1.0 - decay_rate) * (both[0] / FLAT)
    scaled = mean_grad * lax.rsqrt(row_new[:, None] * col_new[None, :])
    sums = jnp.stack([jnp.sum(row_new), jnp.sum(both[1] / row_new)])
    sums = jnp.pad(sums[None], ((0, 0), (0, 126)))
    totals = jnp.sum(share(sums, DP, Q * C), (0, 1))
    row_mean = totals[0] / D
    rms_value = jnp.sqrt(row_mean * totals[1] / (D * FLAT))
    update = scaled * (jnp.sqrt(row_mean) / jnp.maximum(1.0, rms_value))
    stepped = weights - 0.001 * update
    mine = share(stepped, "q", Q)
    other = lax.ppermute(mine, "c", SWAP)
    first = jnp.where(core == 0, mine, other)
    second = jnp.where(core == 0, other, mine)
    new_weights = jnp.stack([first, second], 1).reshape(D, cols)
    return (new_weights, update, row_new, col_new, rms_value)


def solution(mesh):
    split = Mesh(mesh.devices.reshape(Q, C, Z), ("q", "c", "z"))
    in_specs = (P(DP, None, "z"), P(DP, "z"), P(DP), P("z"))
    out_specs = (P(None, "z"), P(DP, "z"), P(DP), P("z"), P())
    return jax.shard_map(
        per_device, mesh=split, in_specs=in_specs, out_specs=out_specs, check_vma=False
    )
```

```python
import jax
import jax.numpy as jnp
from jax import lax
from jax.experimental import pallas as pl
from jax.experimental.pallas import tpu as pltpu
from jax.sharding import Mesh, PartitionSpec as P

D = 4096
STEP = 10
FLAT = 2048
Q, C, Z = 16, 2, 16
ROWS = D // (Q * C)
COLS = FLAT // Z
CHUNKS = 4
DP = ("q", "c")
SWAP = [(0, 1), (1, 0)]
VMEM = pl.BlockSpec(memory_space=pltpu.VMEM)
HBM = pl.BlockSpec(memory_space=pltpu.HBM)
ANY = pl.BlockSpec(memory_space=pl.ANY)


def share(x, axes, n):
    return lax.all_to_all(
        jnp.broadcast_to(x[None], (n, *x.shape)), axes, 0, 0, tiled=True
    )


def sent_body(grads, sent, held, sems):
    core = lax.axis_index("c")
    part = Q // CHUNKS
    copies = []
    for i in range(CHUNKS):
        at = pl.ds(i * part, part)
        copies.append(
            pltpu.make_async_copy(grads.at[at, 1 - core], held.at[at], sems.at[i])
        )
        copies[i].start()
    for i in range(CHUNKS):
        at = pl.ds(i * part, part)
        copies[i].wait()
        sent[at] = held[at].astype(jnp.float32)


def sent_rows(grads):
    shape = (Q, ROWS, COLS)
    return pl.pallas_call(
        sent_body,
        out_shape=jax.ShapeDtypeStruct(shape, jnp.float32),
        in_specs=[HBM],
        out_specs=VMEM,
        scratch_shapes=[
            pltpu.VMEM(shape, grads.dtype),
            pltpu.SemaphoreType.DMA((CHUNKS,)),
        ],
        compiler_params=pltpu.CompilerParams(vmem_limit_bytes=16 * 2**20),
        name="sent_rows",
    )(grads)


def step_body(parts, scaled, weights, update, stepped, rms):
    totals = jnp.sum(jnp.sum(parts[...], 0), 1, keepdims=True)
    row_mean = totals[0:1] / D
    rms_value = jnp.sqrt(row_mean * totals[1:2] / (D * FLAT))
    gain = jnp.sqrt(row_mean) / jnp.maximum(1.0, rms_value)
    new = scaled[...] * gain
    update[...] = new
    after = weights[...] - 0.001 * new
    for i in range(Q):
        stepped[i] = after
    rms[...] = rms_value


def step(parts, scaled, weights):
    return pl.pallas_call(
        step_body,
        out_shape=(
            jax.ShapeDtypeStruct((ROWS, COLS), jnp.float32),
            jax.ShapeDtypeStruct((Q, ROWS, COLS), jnp.float32),
            jax.ShapeDtypeStruct((1, 1), jnp.float32),
        ),
        in_specs=[VMEM, VMEM, VMEM],
        out_specs=(VMEM, VMEM, VMEM),
        compiler_params=pltpu.CompilerParams(vmem_limit_bytes=16 * 2**20),
        name="step",
    )(parts, scaled, weights)


def lay_mine_body(mine, whole, sem):
    copy = pltpu.make_async_copy(mine, whole.at[:, lax.axis_index("c")], sem)
    copy.start()
    copy.wait()


def lay_other_body(other, half, whole, sem):
    copy = pltpu.make_async_copy(other, whole.at[:, 1 - lax.axis_index("c")], sem)
    copy.start()
    copy.wait()


def lay(body, *operands):
    return pl.pallas_call(
        body,
        out_shape=jax.ShapeDtypeStruct((Q, C, ROWS, COLS), jnp.float32),
        in_specs=[ANY, HBM][: len(operands)],
        out_specs=HBM,
        input_output_aliases={1: 0} if len(operands) == 2 else {},
        scratch_shapes=[pltpu.SemaphoreType.DMA],
        compiler_params=pltpu.CompilerParams(vmem_limit_bytes=16 * 2**20),
        cost_estimate=pl.CostEstimate(
            flops=0, bytes_accessed=2 * Q * ROWS * COLS * 4, transcendentals=0
        ),
        name="lay",
    )(*operands)


def per_device(replica_grads, weights, row_state, col_state):
    decay_rate = 1.0 - float(STEP) ** (-0.8)

    grads = replica_grads.reshape(Q, C, ROWS, COLS)
    other = lax.ppermute(sent_rows(grads), "c", SWAP)
    kept = lax.dynamic_index_in_dim(grads, lax.axis_index("c"), 1, False)
    kept = lax.optimization_barrier(kept.astype(jnp.float32))
    chip = kept + other
    mean_grad = jnp.sum(lax.all_to_all(chip, "q", 0, 0, tiled=True), 0) / (Q * C)

    square = mean_grad * mean_grad + 1e-30
    col_sums = jnp.sum(share(jnp.sum(square, 0)[None], DP, Q * C), (0, 1))
    col_new = decay_rate * col_state + (1.0 - decay_rate) * (col_sums / D)
    both = jnp.stack(
        [jnp.sum(square, 1), jnp.sum(mean_grad * mean_grad * (1.0 / col_new), 1)]
    )
    both = jnp.sum(share(both, "z", Z), 0)
    row_new = decay_rate * row_state + (1.0 - decay_rate) * (both[0] / FLAT)
    scaled = mean_grad * lax.rsqrt(row_new[:, None] * col_new[None, :])
    parts = jnp.stack([row_new, both[1] / row_new])
    parts, scaled = lax.optimization_barrier((parts, scaled))
    parts = share(parts, DP, Q * C)
    update, stepped, rms_value = step(parts, scaled, weights)
    mine = lax.all_to_all(stepped, "q", 0, 0, tiled=True)
    other = lax.ppermute(mine, "c", SWAP)
    half = lay(lay_mine_body, mine)
    new_weights = lay(lay_other_body, other, half).reshape(D, COLS)
    return (new_weights, update, row_new, col_new, rms_value.reshape(()))


def solution(mesh):
    split_mesh = Mesh(mesh.devices.reshape(Q, C, Z), ("q", "c", "z"))
    in_specs = (P(DP, None, "z"), P(DP, "z"), P(DP), P("z"))
    out_specs = (P(None, "z"), P(DP, "z"), P(DP), P("z"), P())
    return jax.shard_map(
        per_device,
        mesh=split_mesh,
        in_specs=in_specs,
        out_specs=out_specs,
        check_vma=False,
    )
```

```python
import functools

import jax
import jax.numpy as jnp
from jax import lax
from jax.experimental import pallas as pl
from jax.experimental.pallas import tpu as pltpu
from jax.sharding import Mesh, PartitionSpec as P

D = 4096
STEP = 10
FLAT = 2048
Q, C, Z = 16, 2, 16
ROWS = D // (Q * C)
COLS = FLAT // Z
CHUNKS = 4
AHEAD = (128, 96, 64, 0)
DP = ("q", "c")
SWAP = [(0, 1), (1, 0)]
VMEM = pl.BlockSpec(memory_space=pltpu.VMEM)
HBM = pl.BlockSpec(memory_space=pltpu.HBM)
ANY = pl.BlockSpec(memory_space=pl.ANY)


def share(x, axes, n):
    return lax.all_to_all(
        jnp.broadcast_to(x[None], (n, *x.shape)), axes, 0, 0, tiled=True
    )


def sent_body(grads, sent, held, sems):
    core = lax.axis_index("c")
    part = Q // CHUNKS
    copies = []
    for i in range(CHUNKS):
        at = pl.ds(i * part, part)
        copies.append(
            pltpu.make_async_copy(grads.at[at, 1 - core], held.at[at], sems.at[i])
        )
        copies[i].start()
    for i in range(CHUNKS):
        at = pl.ds(i * part, part)
        copies[i].wait()
        sent[at] = held[at].astype(jnp.float32)


def sent_rows(grads):
    shape = (Q, ROWS, COLS)
    return pl.pallas_call(
        sent_body,
        out_shape=jax.ShapeDtypeStruct(shape, jnp.float32),
        in_specs=[HBM],
        out_specs=VMEM,
        scratch_shapes=[
            pltpu.VMEM(shape, grads.dtype),
            pltpu.SemaphoreType.DMA((CHUNKS,)),
        ],
        compiler_params=pltpu.CompilerParams(vmem_limit_bytes=16 * 2**20),
        name="sent_rows",
    )(grads)


def step_body(parts, scaled, weights, update, stepped, rms):
    totals = jnp.sum(jnp.sum(parts[...], 0), 1, keepdims=True)
    row_mean = totals[0:1] / D
    rms_value = jnp.sqrt(row_mean * totals[1:2] / (D * FLAT))
    gain = jnp.sqrt(row_mean) / jnp.maximum(1.0, rms_value)
    new = scaled[...] * gain
    update[...] = new
    after = weights[...] - 0.001 * new
    for i in range(Q):
        stepped[i] = after
    rms[...] = rms_value


def step(parts, scaled, weights):
    return pl.pallas_call(
        step_body,
        out_shape=(
            jax.ShapeDtypeStruct((ROWS, COLS), jnp.float32),
            jax.ShapeDtypeStruct((Q, ROWS, COLS), jnp.float32),
            jax.ShapeDtypeStruct((1, 1), jnp.float32),
        ),
        in_specs=[VMEM, VMEM, VMEM],
        out_specs=(VMEM, VMEM, VMEM),
        compiler_params=pltpu.CompilerParams(vmem_limit_bytes=16 * 2**20),
        name="step",
    )(parts, scaled, weights)


def lay_body(mine, other, new, rms, row, whole, update, rms_out, row_out, sems):
    core = lax.axis_index("c")
    copies = [
        pltpu.make_async_copy(mine, whole.at[:, core], sems.at[0]),
        pltpu.make_async_copy(other, whole.at[:, 1 - core], sems.at[1]),
        pltpu.make_async_copy(new, update, sems.at[2]),
        pltpu.make_async_copy(rms, rms_out, sems.at[3]),
        pltpu.make_async_copy(row, row_out, sems.at[4]),
    ]
    for copy in copies:
        copy.start()
    for copy in copies:
        copy.wait()


def lay(mine, other, new, rms, row):
    return pl.pallas_call(
        lay_body,
        out_shape=(
            jax.ShapeDtypeStruct((Q, C, ROWS, COLS), jnp.float32),
            jax.ShapeDtypeStruct((ROWS, COLS), jnp.float32),
            jax.ShapeDtypeStruct((1, 1), jnp.float32),
            jax.ShapeDtypeStruct((1, ROWS), jnp.float32),
        ),
        in_specs=[ANY] * 5,
        out_specs=(HBM,) * 4,
        scratch_shapes=[pltpu.SemaphoreType.DMA((5,))],
        compiler_params=pltpu.CompilerParams(vmem_limit_bytes=16 * 2**20),
        name="lay",
    )(mine, other, new, rms, row)


def finish_body(ahead, mine, other, own, others, scaled, row, whole, update, rms, row_out, out, sems):
    core = lax.axis_index("c")
    part = Q // CHUNKS
    tail = pl.ds(ROWS, 8)
    parts = jnp.sum(mine[:, tail], 0) + jnp.sum(other[:, tail], 0)
    totals = jnp.sum(parts[0:2], 1, keepdims=True)
    row_mean = totals[0:1] / D
    rms_value = jnp.sqrt(row_mean * totals[1:2] / (D * FLAT))
    gain = jnp.sqrt(row_mean) / jnp.maximum(1.0, rms_value)
    rms[...] = rms_value
    row_out[...] = row[...]
    lowered = 0.001 * gain
    writes = []
    for i in range(CHUNKS):
        for j in range(i * part, (i + 1) * part):
            for side, rows, known in ((core, mine, own), (1 - core, other, others)):
                out[j, side, :ahead] = known[j] - lowered * rows[j, :ahead]
                if ahead < ROWS:
                    out[j, side, ahead:] = (
                        rows[j, ROWS + 8 :] - lowered * rows[j, ahead:ROWS]
                    )
        at = pl.ds(i * part, part)
        writes.append(pltpu.make_async_copy(out.at[at], whole.at[at], sems.at[i]))
        writes[i].start()
    update[...] = scaled[...] * gain
    for i in range(CHUNKS):
        writes[i].wait()


def finish(ahead, mine, other, own, others, scaled, row):
    whole = (Q, C, ROWS, COLS)
    return pl.pallas_call(
        functools.partial(finish_body, ahead),
        out_shape=(
            jax.ShapeDtypeStruct(whole, jnp.float32),
            jax.ShapeDtypeStruct((ROWS, COLS), jnp.float32),
            jax.ShapeDtypeStruct((1, 1), jnp.float32),
            jax.ShapeDtypeStruct((1, ROWS), jnp.float32),
        ),
        in_specs=[VMEM] * 6,
        out_specs=(HBM, VMEM, VMEM, VMEM),
        scratch_shapes=[
            pltpu.VMEM(whole, jnp.float32),
            pltpu.SemaphoreType.DMA((CHUNKS,)),
        ],
        compiler_params=pltpu.CompilerParams(vmem_limit_bytes=16 * 2**20),
        name="finish",
    )(mine, other, own, others, scaled, row)


def front(ahead, chip, weights):
    sent = chip
    if ahead:
        rows = jnp.broadcast_to(weights[None, :ahead], (Q, ahead, COLS))
        sent = jnp.concatenate([chip, rows], 1)
    got = lax.all_to_all(sent, "q", 0, 0, tiled=True)
    rows = jnp.pad(got[:, ROWS:], ((0, 0), (0, ROWS - ahead), (0, 0)))
    return jnp.sum(got[:, :ROWS], 0) / (Q * C), rows


def back(ahead, scaled, parts, row, weights, own_weights):
    if ahead:
        outs = back_early(ahead, scaled, parts, row, weights, own_weights)
    else:
        outs = back_late(scaled, parts, row, weights)
    return outs[0].reshape(D, COLS), outs[1], outs[2].reshape(()), outs[3][0]


def back_early(ahead, scaled, parts, row, weights, own_weights):
    own = own_weights[:, :ahead]
    others = lax.ppermute(own, "c", SWAP)
    empty = jnp.zeros((6, COLS), jnp.float32)
    mine = share(jnp.concatenate([scaled, parts, empty, weights[ahead:]]), "q", Q)
    other = lax.ppermute(mine, "c", SWAP)
    return finish(ahead, mine, other, own, others, scaled, row)


def back_late(scaled, parts, row, weights):
    parts = share(parts, DP, Q * C)
    new, stepped, rms = step(parts, scaled, weights)
    mine = lax.all_to_all(stepped, "q", 0, 0, tiled=True)
    other = lax.ppermute(mine, "c", SWAP)
    return lay(mine, other, new, rms, row)


def per_device(replica_grads, weights, row_state, col_state):
    decay_rate = 1.0 - float(STEP) ** (-0.8)

    grads = replica_grads.reshape(Q, C, ROWS, COLS)
    other = lax.ppermute(sent_rows(grads), "c", SWAP)
    kept = lax.dynamic_index_in_dim(grads, lax.axis_index("c"), 1, False)
    kept = lax.optimization_barrier(kept.astype(jnp.float32))
    chip = kept + other
    plane = jnp.minimum(lax.axis_index("z") // 2, len(AHEAD) - 1)
    mean_grad, own_weights = lax.switch(
        plane, [functools.partial(front, n) for n in AHEAD], chip, weights
    )

    square = mean_grad * mean_grad + 1e-30
    col_sums = jnp.sum(share(jnp.sum(square, 0)[None], DP, Q * C), (0, 1))
    col_new = decay_rate * col_state + (1.0 - decay_rate) * (col_sums / D)
    both = jnp.stack(
        [jnp.sum(square, 1), jnp.sum(mean_grad * mean_grad * (1.0 / col_new), 1)]
    )
    both = jnp.sum(share(both, "z", Z), 0)
    row_new = decay_rate * row_state + (1.0 - decay_rate) * (both[0] / FLAT)
    scaled = mean_grad * lax.rsqrt(row_new[:, None] * col_new[None, :])
    parts = jnp.stack([row_new, both[1] / row_new])
    new_weights, update, rms_value, row_new = lax.switch(
        plane,
        [functools.partial(back, n) for n in AHEAD],
        *(scaled, parts, row_new[None], weights, own_weights),
    )
    return (new_weights, update, row_new, col_new, rms_value)


def solution(mesh):
    split_mesh = Mesh(mesh.devices.reshape(Q, C, Z), ("q", "c", "z"))
    in_specs = (P(DP, None, "z"), P(DP, "z"), P(DP), P("z"))
    out_specs = (P(None, "z"), P(DP, "z"), P(DP), P("z"), P())
    return jax.shard_map(
        per_device,
        mesh=split_mesh,
        in_specs=in_specs,
        out_specs=out_specs,
        check_vma=False,
    )
```

```python
import functools

import jax
import jax.numpy as jnp
from jax import lax
from jax.experimental import pallas as pl
from jax.experimental.pallas import tpu as pltpu
from jax.sharding import Mesh, PartitionSpec as P

D = 4096
STEP = 10
FLAT = 2048
Q, C, Z = 16, 2, 16
ROWS = D // (Q * C)
COLS = FLAT // Z
AHEAD = (128, 112, 96, 72, 64, 0)
DP = ("q", "c")
SWAP = [(0, 1), (1, 0)]
VMEM = pl.BlockSpec(memory_space=pltpu.VMEM)
HBM = pl.BlockSpec(memory_space=pltpu.HBM)
ANY = pl.BlockSpec(memory_space=pl.ANY)


def share(x, axes, n):
    return lax.all_to_all(
        jnp.broadcast_to(x[None], (n, *x.shape)), axes, 0, 0, tiled=True
    )


def clip(ones, others):
    one, other = ones[0], others[0]
    for i in range(1, Q):
        one, other = one + ones[i], other + others[i]
    totals = jnp.sum(one + other, 1, keepdims=True)
    row_mean = totals[0:1] / D
    rms_value = jnp.sqrt(row_mean * totals[1:2] / (D * FLAT))
    return rms_value, jnp.sqrt(row_mean) / jnp.maximum(1.0, rms_value)


def step_body(parts, scaled, weights, update, stepped, rms):
    rms_value, gain = clip(
        [parts[C * i] for i in range(Q)], [parts[C * i + 1] for i in range(Q)]
    )
    new = scaled[...] * gain
    update[...] = new
    after = weights[...] - 0.001 * new
    for i in range(Q):
        stepped[i] = after
    rms[...] = rms_value


def step(parts, scaled, weights):
    return pl.pallas_call(
        step_body,
        out_shape=(
            jax.ShapeDtypeStruct((ROWS, COLS), jnp.float32),
            jax.ShapeDtypeStruct((Q, ROWS, COLS), jnp.float32),
            jax.ShapeDtypeStruct((1, 1), jnp.float32),
        ),
        in_specs=[VMEM, VMEM, VMEM],
        out_specs=(VMEM, VMEM, VMEM),
        compiler_params=pltpu.CompilerParams(vmem_limit_bytes=16 * 2**20),
        name="step",
    )(parts, scaled, weights)


def copy_all(pairs, sems):
    copies = [
        pltpu.make_async_copy(source, target, sems.at[i])
        for i, (source, target) in enumerate(pairs)
    ]
    for copy in copies:
        copy.start()
    for copy in copies:
        copy.wait()


def small_body(new, rms, row, update, rms_out, row_out, sems):
    copy_all([(new, update), (rms, rms_out), (row, row_out)], sems)


def small(new, rms, row):
    return pl.pallas_call(
        small_body,
        out_shape=(
            jax.ShapeDtypeStruct((ROWS, COLS), jnp.float32),
            jax.ShapeDtypeStruct((1, 1), jnp.float32),
            jax.ShapeDtypeStruct((1, ROWS), jnp.float32),
        ),
        in_specs=[ANY] * 3,
        out_specs=(HBM,) * 3,
        scratch_shapes=[pltpu.SemaphoreType.DMA((3,))],
        compiler_params=pltpu.CompilerParams(vmem_limit_bytes=16 * 2**20),
        cost_estimate=pl.CostEstimate(
            flops=0, bytes_accessed=Q * ROWS * COLS * 4, transcendentals=0
        ),
        name="small",
    )(new, rms, row)


def lay_body(mine, other, whole, sems):
    core = lax.axis_index("c")
    copy_all([(mine, whole.at[:, core]), (other, whole.at[:, 1 - core])], sems)


def lay(mine, other):
    return pl.pallas_call(
        lay_body,
        out_shape=jax.ShapeDtypeStruct((Q, C, ROWS, COLS), jnp.float32),
        in_specs=[ANY] * 2,
        out_specs=HBM,
        scratch_shapes=[pltpu.SemaphoreType.DMA((2,))],
        compiler_params=pltpu.CompilerParams(vmem_limit_bytes=16 * 2**20),
        name="lay",
    )(mine, other)


def finish_body(ahead, mine, other, own, others, scaled, row, *refs):
    whole, update, rms, row_out = refs
    core = lax.axis_index("c")
    tail = pl.ds(ROWS, 8)
    rms_value, gain = clip(
        [mine[i, tail][0:2] for i in range(Q)], [other[i, tail][0:2] for i in range(Q)]
    )
    rms[...] = rms_value
    update[...] = scaled[...] * gain
    row_out[...] = row[...]
    lowered = 0.001 * gain
    for j in range(Q):
        for side, rows, known in ((core, mine, own), (1 - core, other, others)):
            whole[j, side, :ahead] = known[j] - lowered * rows[j, :ahead]
            if ahead < ROWS:
                whole[j, side, ahead:] = (
                    rows[j, ROWS + 8 :] - lowered * rows[j, ahead:ROWS]
                )


def finish(ahead, mine, other, own, others, scaled, row):
    whole = (Q, C, ROWS, COLS)
    return pl.pallas_call(
        functools.partial(finish_body, ahead),
        out_shape=(
            jax.ShapeDtypeStruct(whole, jnp.float32),
            jax.ShapeDtypeStruct((ROWS, COLS), jnp.float32),
            jax.ShapeDtypeStruct((1, 1), jnp.float32),
            jax.ShapeDtypeStruct((1, ROWS), jnp.float32),
        ),
        in_specs=[VMEM] * 6,
        out_specs=(VMEM,) * 4,
        compiler_params=pltpu.CompilerParams(vmem_limit_bytes=16 * 2**20),
        name="finish",
    )(mine, other, own, others, scaled, row)


def front(ahead, chip, weights):
    sent = chip
    if ahead:
        rows = jnp.broadcast_to(weights[None, :ahead], (Q, ahead, COLS))
        sent = jnp.concatenate([chip, rows], 1)
    got = lax.all_to_all(sent, "q", 0, 0, tiled=True)
    rows = jnp.pad(got[:, ROWS:], ((0, 0), (0, ROWS - ahead), (0, 0)))
    return jnp.sum(got[:, :ROWS], 0) / (Q * C), rows


def back(ahead, scaled, parts, row, weights, own_weights):
    if ahead:
        outs = back_early(ahead, scaled, parts, row, weights, own_weights)
    else:
        outs = back_late(scaled, parts, row, weights)
    return outs[0].reshape(D, COLS), outs[1], outs[2].reshape(()), outs[3][0]


def back_early(ahead, scaled, parts, row, weights, own_weights):
    own = own_weights[:, :ahead]
    others = lax.ppermute(own, "c", SWAP)
    empty = jnp.zeros((6, COLS), jnp.float32)
    mine = share(jnp.concatenate([scaled, parts, empty, weights[ahead:]]), "q", Q)
    other = lax.ppermute(mine, "c", SWAP)
    return finish(ahead, mine, other, own, others, scaled, row)


def back_late(scaled, parts, row, weights):
    parts = share(parts, DP, Q * C)
    new, stepped, rms = step(parts, scaled, weights)
    mine = lax.all_to_all(stepped, "q", 0, 0, tiled=True)
    mine, new, rms, row = lax.optimization_barrier((mine, new, rms, row))
    other = lax.ppermute(mine, "c", SWAP)
    update, rms, row = small(new, rms, row)
    return lay(mine, other), update, rms, row


def per_device(replica_grads, weights, row_state, col_state):
    decay_rate = 1.0 - float(STEP) ** (-0.8)

    grads = replica_grads.reshape(Q, C, ROWS, COLS)
    core = lax.axis_index("c")
    sent = lax.dynamic_index_in_dim(grads, 1 - core, 1, False).astype(jnp.float32)
    sent, grads = lax.optimization_barrier((sent, grads))
    other = lax.ppermute(sent, "c", SWAP)
    kept = lax.dynamic_index_in_dim(grads, core, 1, False)
    kept = lax.optimization_barrier(kept.astype(jnp.float32))
    chip = kept + other
    plane = jnp.clip(lax.axis_index("z") - 1, 0, len(AHEAD) - 1)
    mean_grad, own_weights = lax.switch(
        plane, [functools.partial(front, n) for n in AHEAD], chip, weights
    )

    square = mean_grad * mean_grad + 1e-30
    col_sums = jnp.sum(share(jnp.sum(square, 0)[None], DP, Q * C), (0, 1))
    col_new = decay_rate * col_state + (1.0 - decay_rate) * (col_sums / D)
    both = jnp.stack(
        [jnp.sum(square, 1), jnp.sum(mean_grad * mean_grad * (1.0 / col_new), 1)]
    )
    both = jnp.sum(share(both, "z", Z), 0)
    row_new = decay_rate * row_state + (1.0 - decay_rate) * (both[0] / FLAT)
    scaled = mean_grad * lax.rsqrt(row_new[:, None] * col_new[None, :])
    parts = jnp.stack([row_new, both[1] / row_new])
    new_weights, update, rms_value, row_new = lax.switch(
        plane,
        [functools.partial(back, n) for n in AHEAD],
        *(scaled, parts, row_new[None], weights, own_weights),
    )
    return (new_weights, update, row_new, col_new, rms_value)


def solution(mesh):
    split_mesh = Mesh(mesh.devices.reshape(Q, C, Z), ("q", "c", "z"))
    in_specs = (P(DP, None, "z"), P(DP, "z"), P(DP), P("z"))
    out_specs = (P(None, "z"), P(DP, "z"), P(DP), P("z"), P())
    return jax.shard_map(
        per_device,
        mesh=split_mesh,
        in_specs=in_specs,
        out_specs=out_specs,
        check_vma=False,
    )
```

```python
import functools

import jax
import jax.numpy as jnp
from jax import lax
from jax.experimental import pallas as pl
from jax.experimental.pallas import tpu as pltpu
from jax.sharding import Mesh, PartitionSpec as P

D = 4096
STEP = 10
FLAT = 2048
Q, C, Z = 16, 2, 16
ROWS = D // (Q * C)
COLS = FLAT // Z
AHEAD = (128, 112, 80, 56, 0)
SIDE = range(4)
ALONG_X = [[[(y * 4 + x) * C + c for x in SIDE] for y in SIDE] for c in range(C)]
ALONG_Y = [[[(y * 4 + x) * C + c for y in SIDE] for x in SIDE] for c in range(C)]
FIRST = ALONG_X[0] + ALONG_Y[1]
SECOND = ALONG_Y[0] + ALONG_X[1]
DP = ("q", "c")
SWAP = [(0, 1), (1, 0)]
VMEM = pl.BlockSpec(memory_space=pltpu.VMEM)
HBM = pl.BlockSpec(memory_space=pltpu.HBM)
ANY = pl.BlockSpec(memory_space=pl.ANY)


def share(x, axes, n):
    return lax.all_to_all(
        jnp.broadcast_to(x[None], (n, *x.shape)), axes, 0, 0, tiled=True
    )


def clip(ones, others):
    one, other = ones[0], others[0]
    for i in range(1, Q):
        one, other = one + ones[i], other + others[i]
    totals = jnp.sum(one + other, 1, keepdims=True)
    row_mean = totals[0:1] / D
    rms_value = jnp.sqrt(row_mean * totals[1:2] / (D * FLAT))
    return rms_value, jnp.sqrt(row_mean) / jnp.maximum(1.0, rms_value)


def step_body(parts, scaled, weights, update, stepped, rms):
    rms_value, gain = clip(
        [parts[C * i] for i in range(Q)], [parts[C * i + 1] for i in range(Q)]
    )
    new = scaled[...] * gain
    update[...] = new
    after = weights[...] - 0.001 * new
    for i in range(Q):
        stepped[i] = after
    rms[...] = rms_value


def step(parts, scaled, weights):
    return pl.pallas_call(
        step_body,
        out_shape=(
            jax.ShapeDtypeStruct((ROWS, COLS), jnp.float32),
            jax.ShapeDtypeStruct((Q, ROWS, COLS), jnp.float32),
            jax.ShapeDtypeStruct((1, 1), jnp.float32),
        ),
        in_specs=[VMEM, VMEM, VMEM],
        out_specs=(VMEM, VMEM, VMEM),
        compiler_params=pltpu.CompilerParams(vmem_limit_bytes=16 * 2**20),
        name="step",
    )(parts, scaled, weights)


def copy_all(pairs, sems):
    copies = [
        pltpu.make_async_copy(source, target, sems.at[i])
        for i, (source, target) in enumerate(pairs)
    ]
    for copy in copies:
        copy.start()
    for copy in copies:
        copy.wait()


def small_body(new, rms, row, update, rms_out, row_out, sems):
    copy_all([(new, update), (rms, rms_out), (row, row_out)], sems)


def small(new, rms, row):
    return pl.pallas_call(
        small_body,
        out_shape=(
            jax.ShapeDtypeStruct((ROWS, COLS), jnp.float32),
            jax.ShapeDtypeStruct((1, 1), jnp.float32),
            jax.ShapeDtypeStruct((1, ROWS), jnp.float32),
        ),
        in_specs=[ANY] * 3,
        out_specs=(HBM,) * 3,
        scratch_shapes=[pltpu.SemaphoreType.DMA((3,))],
        compiler_params=pltpu.CompilerParams(vmem_limit_bytes=16 * 2**20),
        cost_estimate=pl.CostEstimate(
            flops=0, bytes_accessed=Q * ROWS * COLS * 4, transcendentals=0
        ),
        name="small",
    )(new, rms, row)


def lay_body(mine, other, whole, sems):
    core = lax.axis_index("c")
    copy_all([(mine, whole.at[:, core]), (other, whole.at[:, 1 - core])], sems)


def lay(mine, other):
    return pl.pallas_call(
        lay_body,
        out_shape=jax.ShapeDtypeStruct((Q, C, ROWS, COLS), jnp.float32),
        in_specs=[ANY] * 2,
        out_specs=HBM,
        scratch_shapes=[pltpu.SemaphoreType.DMA((2,))],
        compiler_params=pltpu.CompilerParams(vmem_limit_bytes=16 * 2**20),
        name="lay",
    )(mine, other)


def finish_body(ahead, mine, other, own, others, scaled, row, *refs):
    whole, update, rms, row_out = refs
    core = lax.axis_index("c")
    tail = pl.ds(ROWS, 8)
    rms_value, gain = clip(
        [mine[i, tail][0:2] for i in range(Q)], [other[i, tail][0:2] for i in range(Q)]
    )
    rms[...] = rms_value
    update[...] = scaled[...] * gain
    row_out[...] = row[...]
    lowered = 0.001 * gain
    for j in range(Q):
        for side, rows, known in ((core, mine, own), (1 - core, other, others)):
            at = jnp.where(side == 0, j, j % 4 * 4 + j // 4)
            whole[j, side, :ahead] = known[at, :ahead] - lowered * rows[j, :ahead]
            if ahead < ROWS:
                whole[j, side, ahead:] = (
                    rows[j, ROWS + 8 :] - lowered * rows[j, ahead:ROWS]
                )


def finish(ahead, mine, other, own, others, scaled, row):
    whole = (Q, C, ROWS, COLS)
    return pl.pallas_call(
        functools.partial(finish_body, ahead),
        out_shape=(
            jax.ShapeDtypeStruct(whole, jnp.float32),
            jax.ShapeDtypeStruct((ROWS, COLS), jnp.float32),
            jax.ShapeDtypeStruct((1, 1), jnp.float32),
            jax.ShapeDtypeStruct((1, ROWS), jnp.float32),
        ),
        in_specs=[VMEM] * 6,
        out_specs=(VMEM,) * 4,
        compiler_params=pltpu.CompilerParams(vmem_limit_bytes=16 * 2**20),
        name="finish",
    )(mine, other, own, others, scaled, row)


def arrange_body(ahead, kept, other, weights, out):
    turn = lax.axis_index("c") == 0
    for i in range(4):
        for j in range(4):
            at = jnp.where(turn, j * 4 + i, i * 4 + j)
            out[i, j * ROWS : (j + 1) * ROWS] = kept[at] + other[at]
        out[i, 4 * ROWS :] = weights[:ahead]


def arrange(ahead, kept, other, weights):
    return pl.pallas_call(
        functools.partial(arrange_body, ahead),
        out_shape=jax.ShapeDtypeStruct((4, 4 * ROWS + ahead, COLS), jnp.float32),
        in_specs=[VMEM] * 3,
        out_specs=VMEM,
        compiler_params=pltpu.CompilerParams(vmem_limit_bytes=16 * 2**20),
        name="arrange",
    )(kept, other, weights)


def column_sums(mean_grad):
    square = mean_grad * mean_grad + 1e-30
    return jnp.sum(share(jnp.sum(square, 0)[None], DP, Q * C), (0, 1))


def front(ahead, kept, other, weights):
    if not ahead:
        got = lax.all_to_all(kept + other, "q", 0, 0, tiled=True)
        mean_grad = jnp.sum(got, 0) / (Q * C)
        none = jnp.zeros((Q, ROWS, COLS), jnp.float32)
        return mean_grad, column_sums(mean_grad), none, none

    def exchange(x, groups):
        return lax.all_to_all(x, DP, 0, 0, axis_index_groups=groups, tiled=True)

    got = exchange(arrange(ahead, kept, other, weights), FIRST)
    sums = jnp.sum(got[:, : 4 * ROWS], 0).reshape(4, ROWS, COLS)
    rows = got[:, 4 * ROWS :].reshape(1, 4 * ahead, COLS)
    rows = jnp.broadcast_to(rows, (4, 4 * ahead, COLS))
    got = exchange(jnp.concatenate([sums, rows], 1), SECOND)
    mean_grad = jnp.sum(got[:, :ROWS], 0) / (Q * C)
    rows = got[:, ROWS:].reshape(Q, ahead, COLS)
    if ahead < ROWS:
        rows = jnp.pad(rows, ((0, 0), (0, ROWS - ahead), (0, 0)))
        others = jnp.zeros_like(rows)
    else:
        others = lax.ppermute(rows, "c", SWAP)
    return mean_grad, column_sums(mean_grad), rows, others


def back(ahead, scaled, parts, row, weights, own, others):
    if ahead:
        outs = back_early(ahead, scaled, parts, row, weights, own, others)
    else:
        outs = back_late(scaled, parts, row, weights)
    return outs[0].reshape(D, COLS), outs[1], outs[2].reshape(()), outs[3][0]


def back_early(ahead, scaled, parts, row, weights, own, others):
    if ahead < ROWS:
        own = own[:, :ahead]
        others = lax.ppermute(own, "c", SWAP)
    empty = jnp.zeros((6, COLS), jnp.float32)
    mine = share(jnp.concatenate([scaled, parts, empty, weights[ahead:]]), "q", Q)
    other = lax.ppermute(mine, "c", SWAP)
    return finish(ahead, mine, other, own, others, scaled, row)


def back_late(scaled, parts, row, weights):
    parts = share(parts, DP, Q * C)
    new, stepped, rms = step(parts, scaled, weights)
    mine = lax.all_to_all(stepped, "q", 0, 0, tiled=True)
    mine, new, rms, row = lax.optimization_barrier((mine, new, rms, row))
    other = lax.ppermute(mine, "c", SWAP)
    update, rms, row = small(new, rms, row)
    return lay(mine, other), update, rms, row


def per_device(replica_grads, weights, row_state, col_state):
    decay_rate = 1.0 - float(STEP) ** (-0.8)

    grads = replica_grads.reshape(Q, C, ROWS, COLS)
    core = lax.axis_index("c")
    sent = lax.dynamic_index_in_dim(grads, 1 - core, 1, False).astype(jnp.float32)
    sent, grads = lax.optimization_barrier((sent, grads))
    other = lax.ppermute(sent, "c", SWAP)
    kept = lax.dynamic_index_in_dim(grads, core, 1, False)
    kept = lax.optimization_barrier(kept.astype(jnp.float32))
    plane = jnp.clip(lax.axis_index("z") - 2, 0, len(AHEAD) - 1)
    mean_grad, col_sums, own, others = lax.switch(
        plane, [functools.partial(front, n) for n in AHEAD], kept, other, weights
    )

    square = mean_grad * mean_grad + 1e-30
    col_new = decay_rate * col_state + (1.0 - decay_rate) * (col_sums / D)
    both = jnp.stack(
        [jnp.sum(square, 1), jnp.sum(mean_grad * mean_grad * (1.0 / col_new), 1)]
    )
    both = jnp.sum(share(both, "z", Z), 0)
    row_new = decay_rate * row_state + (1.0 - decay_rate) * (both[0] / FLAT)
    scaled = mean_grad * lax.rsqrt(row_new[:, None] * col_new[None, :])
    parts = jnp.stack([row_new, both[1] / row_new])
    new_weights, update, rms_value, row_new = lax.switch(
        plane,
        [functools.partial(back, n) for n in AHEAD],
        *(scaled, parts, row_new[None], weights, own, others),
    )
    return (new_weights, update, row_new, col_new, rms_value)


def solution(mesh):
    split_mesh = Mesh(mesh.devices.reshape(Q, C, Z), ("q", "c", "z"))
    in_specs = (P(DP, None, "z"), P(DP, "z"), P(DP), P("z"))
    out_specs = (P(None, "z"), P(DP, "z"), P(DP), P("z"), P())
    return jax.shard_map(
        per_device,
        mesh=split_mesh,
        in_specs=in_specs,
        out_specs=out_specs,
        check_vma=False,
    )
```

```python
import functools

import jax
import jax.numpy as jnp
from jax import lax
from jax.experimental import pallas as pl
from jax.experimental.pallas import tpu as pltpu
from jax.sharding import Mesh, PartitionSpec as P

D = 4096
STEP = 10
FLAT = 2048
Q, C, Z = 16, 2, 16
ROWS = D // (Q * C)
COLS = FLAT // Z
AHEAD = (128, 112, 80, 56, 0)
SIDE = range(4)
ALONG_X = [[[(y * 4 + x) * C + c for x in SIDE] for y in SIDE] for c in range(C)]
ALONG_Y = [[[(y * 4 + x) * C + c for y in SIDE] for x in SIDE] for c in range(C)]
FIRST = ALONG_X[0] + ALONG_Y[1]
SECOND = ALONG_Y[0] + ALONG_X[1]
DP = ("q", "c")
SWAP = [(0, 1), (1, 0)]
VMEM = pl.BlockSpec(memory_space=pltpu.VMEM)
HBM = pl.BlockSpec(memory_space=pltpu.HBM)
ANY = pl.BlockSpec(memory_space=pl.ANY)


def share(x, axes, n):
    return lax.all_to_all(
        jnp.broadcast_to(x[None], (n, *x.shape)), axes, 0, 0, tiled=True
    )


def clip(ones, others):
    one, other = ones[0], others[0]
    for i in range(1, Q):
        one, other = one + ones[i], other + others[i]
    totals = jnp.sum(one + other, 1, keepdims=True)
    row_mean = totals[0:1] / D
    rms_value = jnp.sqrt(row_mean * totals[1:2] / (D * FLAT))
    return rms_value, jnp.sqrt(row_mean) / jnp.maximum(1.0, rms_value)


def step_body(parts, scaled, weights, update, stepped, rms):
    rms_value, gain = clip(
        [parts[C * i] for i in range(Q)], [parts[C * i + 1] for i in range(Q)]
    )
    new = scaled[...] * gain
    update[...] = new
    after = weights[...] - 0.001 * new
    for i in range(Q):
        stepped[i] = after
    rms[...] = rms_value


def step(parts, scaled, weights):
    return pl.pallas_call(
        step_body,
        out_shape=(
            jax.ShapeDtypeStruct((ROWS, COLS), jnp.float32),
            jax.ShapeDtypeStruct((Q, ROWS, COLS), jnp.float32),
            jax.ShapeDtypeStruct((1, 1), jnp.float32),
        ),
        in_specs=[VMEM, VMEM, VMEM],
        out_specs=(VMEM, VMEM, VMEM),
        compiler_params=pltpu.CompilerParams(vmem_limit_bytes=16 * 2**20),
        name="step",
    )(parts, scaled, weights)


def copy_all(pairs, sems):
    copies = [
        pltpu.make_async_copy(source, target, sems.at[i])
        for i, (source, target) in enumerate(pairs)
    ]
    for copy in copies:
        copy.start()
    for copy in copies:
        copy.wait()


def small_body(new, rms, row, update, rms_out, row_out, sems):
    copy_all([(new, update), (rms, rms_out), (row, row_out)], sems)


def small(new, rms, row):
    return pl.pallas_call(
        small_body,
        out_shape=(
            jax.ShapeDtypeStruct((ROWS, COLS), jnp.float32),
            jax.ShapeDtypeStruct((1, 1), jnp.float32),
            jax.ShapeDtypeStruct((1, ROWS), jnp.float32),
        ),
        in_specs=[ANY] * 3,
        out_specs=(HBM,) * 3,
        scratch_shapes=[pltpu.SemaphoreType.DMA((3,))],
        compiler_params=pltpu.CompilerParams(vmem_limit_bytes=16 * 2**20),
        cost_estimate=pl.CostEstimate(
            flops=0, bytes_accessed=Q * ROWS * COLS * 4, transcendentals=0
        ),
        name="small",
    )(new, rms, row)


def lay_body(mine, other, whole, sems):
    core = lax.axis_index("c")
    copy_all([(mine, whole.at[:, core]), (other, whole.at[:, 1 - core])], sems)


def lay(mine, other):
    return pl.pallas_call(
        lay_body,
        out_shape=jax.ShapeDtypeStruct((Q, C, ROWS, COLS), jnp.float32),
        in_specs=[ANY] * 2,
        out_specs=HBM,
        scratch_shapes=[pltpu.SemaphoreType.DMA((2,))],
        compiler_params=pltpu.CompilerParams(vmem_limit_bytes=16 * 2**20),
        name="lay",
    )(mine, other)


def finish_body(ahead, mine, other, own, others, scaled, row, *refs):
    whole, update, rms, row_out = refs
    core = lax.axis_index("c")
    tail = pl.ds(ROWS, 8)
    rms_value, gain = clip(
        [mine[i, tail][0:2] for i in range(Q)], [other[i, tail][0:2] for i in range(Q)]
    )
    rms[...] = rms_value
    update[...] = scaled[...] * gain
    row_out[...] = row[...]
    lowered = 0.001 * gain
    for j in range(Q):
        for side, rows, known in ((core, mine, own), (1 - core, other, others)):
            at = jnp.where(side == 0, j, j % 4 * 4 + j // 4)
            whole[j, side, :ahead] = known[at, :ahead] - lowered * rows[j, :ahead]
            if ahead < ROWS:
                whole[j, side, ahead:] = (
                    rows[j, ROWS + 8 :] - lowered * rows[j, ahead:ROWS]
                )


def finish(ahead, mine, other, own, others, scaled, row):
    whole = (Q, C, ROWS, COLS)
    return pl.pallas_call(
        functools.partial(finish_body, ahead),
        out_shape=(
            jax.ShapeDtypeStruct(whole, jnp.float32),
            jax.ShapeDtypeStruct((ROWS, COLS), jnp.float32),
            jax.ShapeDtypeStruct((1, 1), jnp.float32),
            jax.ShapeDtypeStruct((1, ROWS), jnp.float32),
        ),
        in_specs=[VMEM] * 6,
        out_specs=(VMEM,) * 4,
        compiler_params=pltpu.CompilerParams(vmem_limit_bytes=16 * 2**20),
        name="finish",
    )(mine, other, own, others, scaled, row)


def arrange_body(ahead, kept, other, weights, out):
    turn = lax.axis_index("c") == 0
    for i in range(4):
        for j in range(4):
            at = jnp.where(turn, j * 4 + i, i * 4 + j)
            out[i, j * ROWS : (j + 1) * ROWS] = kept[at] + other[at]
        out[i, 4 * ROWS :] = weights[:ahead]


def arrange(ahead, kept, other, weights):
    return pl.pallas_call(
        functools.partial(arrange_body, ahead),
        out_shape=jax.ShapeDtypeStruct((4, 4 * ROWS + ahead, COLS), jnp.float32),
        in_specs=[VMEM] * 3,
        out_specs=VMEM,
        compiler_params=pltpu.CompilerParams(vmem_limit_bytes=16 * 2**20),
        name="arrange",
    )(kept, other, weights)


def column_sums(mean_grad):
    square = mean_grad * mean_grad + 1e-30
    return share(jnp.sum(square, 0)[None], DP, Q * C)


def front(ahead, kept, other, weights):
    if not ahead:
        got = lax.all_to_all(kept + other, "q", 0, 0, tiled=True)
        mean_grad = jnp.sum(got, 0) / (Q * C)
        col_sums = column_sums(mean_grad)
        none = jnp.broadcast_to(col_sums[:Q], (Q, ROWS, COLS))
        return mean_grad, col_sums, none, none

    def exchange(x, groups):
        return lax.all_to_all(x, DP, 0, 0, axis_index_groups=groups, tiled=True)

    got = exchange(arrange(ahead, kept, other, weights), FIRST)
    sums = jnp.sum(got[:, : 4 * ROWS], 0).reshape(4, ROWS, COLS)
    rows = got[:, 4 * ROWS :].reshape(1, 4 * ahead, COLS)
    rows = jnp.broadcast_to(rows, (4, 4 * ahead, COLS))
    got = exchange(jnp.concatenate([sums, rows], 1), SECOND)
    mean_grad = jnp.sum(got[:, :ROWS], 0) / (Q * C)
    rows = got[:, ROWS:].reshape(Q, ahead, COLS)
    if ahead < ROWS:
        rows = jnp.pad(rows, ((0, 0), (0, ROWS - ahead), (0, 0)))
        others = jnp.zeros_like(rows)
    else:
        others = lax.ppermute(rows, "c", SWAP)
    return mean_grad, column_sums(mean_grad), rows, others


def back(ahead, scaled, parts, row, weights, own, others):
    if ahead:
        outs = back_early(ahead, scaled, parts, row, weights, own, others)
    else:
        outs = back_late(scaled, parts, row, weights)
    return outs[0].reshape(D, COLS), outs[1], outs[2].reshape(()), outs[3][0]


def back_early(ahead, scaled, parts, row, weights, own, others):
    if ahead < ROWS:
        own = own[:, :ahead]
        others = lax.ppermute(own, "c", SWAP)
    empty = jnp.zeros((6, COLS), jnp.float32)
    mine = share(jnp.concatenate([scaled, parts, empty, weights[ahead:]]), "q", Q)
    other = lax.ppermute(mine, "c", SWAP)
    return finish(ahead, mine, other, own, others, scaled, row)


def back_late(scaled, parts, row, weights):
    parts = share(parts, DP, Q * C)
    new, stepped, rms = step(parts, scaled, weights)
    mine = lax.all_to_all(stepped, "q", 0, 0, tiled=True)
    mine, new, rms, row = lax.optimization_barrier((mine, new, rms, row))
    other = lax.ppermute(mine, "c", SWAP)
    update, rms, row = small(new, rms, row)
    return lay(mine, other), update, rms, row


def per_device(replica_grads, weights, row_state, col_state):
    decay_rate = 1.0 - float(STEP) ** (-0.8)

    grads = replica_grads.reshape(Q, C, ROWS, COLS)
    core = lax.axis_index("c")
    sent = lax.dynamic_index_in_dim(grads, 1 - core, 1, False).astype(jnp.float32)
    sent, grads = lax.optimization_barrier((sent, grads))
    other = lax.ppermute(sent, "c", SWAP)
    kept = lax.dynamic_index_in_dim(grads, core, 1, False)
    kept = lax.optimization_barrier(kept.astype(jnp.float32))
    plane = jnp.clip(lax.axis_index("z") - 2, 0, len(AHEAD) - 1)
    mean_grad, col_sums, own, others = lax.switch(
        plane, [functools.partial(front, n) for n in AHEAD], kept, other, weights
    )

    square = mean_grad * mean_grad + 1e-30
    col_sums = jnp.sum(col_sums, (0, 1))
    col_new = decay_rate * col_state + (1.0 - decay_rate) * (col_sums / D)
    both = jnp.stack(
        [jnp.sum(square, 1), jnp.sum(mean_grad * mean_grad * (1.0 / col_new), 1)]
    )
    both = jnp.sum(share(both, "z", Z), 0)
    row_new = decay_rate * row_state + (1.0 - decay_rate) * (both[0] / FLAT)
    scaled = mean_grad * lax.rsqrt(row_new[:, None] * col_new[None, :])
    parts = jnp.stack([row_new, both[1] / row_new])
    new_weights, update, rms_value, row_new = lax.switch(
        plane,
        [functools.partial(back, n) for n in AHEAD],
        *(scaled, parts, row_new[None], weights, own, others),
    )
    return (new_weights, update, row_new, col_new, rms_value)


def solution(mesh):
    split_mesh = Mesh(mesh.devices.reshape(Q, C, Z), ("q", "c", "z"))
    in_specs = (P(DP, None, "z"), P(DP, "z"), P(DP), P("z"))
    out_specs = (P(None, "z"), P(DP, "z"), P(DP), P("z"), P())
    return jax.shard_map(
        per_device,
        mesh=split_mesh,
        in_specs=in_specs,
        out_specs=out_specs,
        check_vma=False,
    )
```

```python
import functools

import jax
import jax.numpy as jnp
from jax import lax
from jax.experimental import pallas as pl
from jax.experimental.pallas import tpu as pltpu
from jax.sharding import Mesh, PartitionSpec as P

D = 4096
STEP = 10
FLAT = 2048
Q, C, Z = 16, 2, 16
ROWS = D // (Q * C)
COLS = FLAT // Z
AHEAD = (128, 112, 64, 40, 0)
SIDE = range(4)
ALONG_X = [[[(y * 4 + x) * C + c for x in SIDE] for y in SIDE] for c in range(C)]
ALONG_Y = [[[(y * 4 + x) * C + c for y in SIDE] for x in SIDE] for c in range(C)]
FIRST = ALONG_X[0] + ALONG_Y[1]
SECOND = ALONG_Y[0] + ALONG_X[1]
DP = ("q", "c")
SWAP = [(0, 1), (1, 0)]
VMEM = pl.BlockSpec(memory_space=pltpu.VMEM)
HBM = pl.BlockSpec(memory_space=pltpu.HBM)
ANY = pl.BlockSpec(memory_space=pl.ANY)


def share(x, axes, n):
    return lax.all_to_all(
        jnp.broadcast_to(x[None], (n, *x.shape)), axes, 0, 0, tiled=True
    )


def clip(ones, others):
    one, other = ones[0], others[0]
    for i in range(1, Q):
        one, other = one + ones[i], other + others[i]
    totals = jnp.sum(one + other, 1, keepdims=True)
    row_mean = totals[0:1] / D
    rms_value = jnp.sqrt(row_mean * totals[1:2] / (D * FLAT))
    return rms_value, jnp.sqrt(row_mean) / jnp.maximum(1.0, rms_value)


def step_body(parts, scaled, weights, update, stepped, rms):
    rms_value, gain = clip(
        [parts[C * i] for i in range(Q)], [parts[C * i + 1] for i in range(Q)]
    )
    new = scaled[...] * gain
    update[...] = new
    after = weights[...] - 0.001 * new
    for i in range(Q):
        stepped[i] = after
    rms[...] = rms_value


def step(parts, scaled, weights):
    return pl.pallas_call(
        step_body,
        out_shape=(
            jax.ShapeDtypeStruct((ROWS, COLS), jnp.float32),
            jax.ShapeDtypeStruct((Q, ROWS, COLS), jnp.float32),
            jax.ShapeDtypeStruct((1, 1), jnp.float32),
        ),
        in_specs=[VMEM, VMEM, VMEM],
        out_specs=(VMEM, VMEM, VMEM),
        compiler_params=pltpu.CompilerParams(vmem_limit_bytes=16 * 2**20),
        name="step",
    )(parts, scaled, weights)


def copy_all(pairs, sems):
    copies = [
        pltpu.make_async_copy(source, target, sems.at[i])
        for i, (source, target) in enumerate(pairs)
    ]
    for copy in copies:
        copy.start()
    for copy in copies:
        copy.wait()


def small_body(new, rms, row, update, rms_out, row_out, sems):
    copy_all([(new, update), (rms, rms_out), (row, row_out)], sems)


def small(new, rms, row):
    return pl.pallas_call(
        small_body,
        out_shape=(
            jax.ShapeDtypeStruct((ROWS, COLS), jnp.float32),
            jax.ShapeDtypeStruct((1, 1), jnp.float32),
            jax.ShapeDtypeStruct((1, ROWS), jnp.float32),
        ),
        in_specs=[ANY] * 3,
        out_specs=(HBM,) * 3,
        scratch_shapes=[pltpu.SemaphoreType.DMA((3,))],
        compiler_params=pltpu.CompilerParams(vmem_limit_bytes=16 * 2**20),
        cost_estimate=pl.CostEstimate(
            flops=0, bytes_accessed=Q * ROWS * COLS * 4, transcendentals=0
        ),
        name="small",
    )(new, rms, row)


def lay_body(mine, other, whole, sems):
    core = lax.axis_index("c")
    copy_all([(mine, whole.at[:, core]), (other, whole.at[:, 1 - core])], sems)


def lay(mine, other):
    return pl.pallas_call(
        lay_body,
        out_shape=jax.ShapeDtypeStruct((Q, C, ROWS, COLS), jnp.float32),
        in_specs=[ANY] * 2,
        out_specs=HBM,
        scratch_shapes=[pltpu.SemaphoreType.DMA((2,))],
        compiler_params=pltpu.CompilerParams(vmem_limit_bytes=16 * 2**20),
        name="lay",
    )(mine, other)


def finish_body(ahead, mine, other, own, others, scaled, row, *refs):
    whole, update, rms, row_out = refs
    core = lax.axis_index("c")
    tail = pl.ds(ROWS, 8)
    rms_value, gain = clip(
        [mine[i, tail][0:2] for i in range(Q)], [other[i, tail][0:2] for i in range(Q)]
    )
    rms[...] = rms_value
    update[...] = scaled[...] * gain
    row_out[...] = row[...]
    lowered = 0.001 * gain
    for j in range(Q):
        for side, rows, known in ((core, mine, own), (1 - core, other, others)):
            at = jnp.where(side == 0, j, j % 4 * 4 + j // 4)
            whole[j, side, :ahead] = known[at, :ahead] - lowered * rows[j, :ahead]
            if ahead < ROWS:
                whole[j, side, ahead:] = (
                    rows[j, ROWS + 8 :] - lowered * rows[j, ahead:ROWS]
                )


def finish(ahead, mine, other, own, others, scaled, row):
    whole = (Q, C, ROWS, COLS)
    return pl.pallas_call(
        functools.partial(finish_body, ahead),
        out_shape=(
            jax.ShapeDtypeStruct(whole, jnp.float32),
            jax.ShapeDtypeStruct((ROWS, COLS), jnp.float32),
            jax.ShapeDtypeStruct((1, 1), jnp.float32),
            jax.ShapeDtypeStruct((1, ROWS), jnp.float32),
        ),
        in_specs=[VMEM] * 6,
        out_specs=(VMEM,) * 4,
        compiler_params=pltpu.CompilerParams(vmem_limit_bytes=16 * 2**20),
        name="finish",
    )(mine, other, own, others, scaled, row)


def arrange_body(ahead, kept, other, weights, out):
    turn = lax.axis_index("c") == 0
    for i in range(4):
        for j in range(4):
            at = jnp.where(turn, j * 4 + i, i * 4 + j)
            out[i, j * ROWS : (j + 1) * ROWS] = kept[at] + other[at]
        out[i, 4 * ROWS :] = weights[:ahead]


def arrange(ahead, kept, other, weights):
    return pl.pallas_call(
        functools.partial(arrange_body, ahead),
        out_shape=jax.ShapeDtypeStruct((4, 4 * ROWS + ahead, COLS), jnp.float32),
        in_specs=[VMEM] * 3,
        out_specs=VMEM,
        compiler_params=pltpu.CompilerParams(vmem_limit_bytes=16 * 2**20),
        name="arrange",
    )(kept, other, weights)


def column_sums(mean_grad):
    square = mean_grad * mean_grad + 1e-30
    return share(jnp.sum(square, 0)[None], DP, Q * C)


def front(ahead, kept, other, weights):
    if not ahead:
        got = lax.all_to_all(kept + other, "q", 0, 0, tiled=True)
        mean_grad = jnp.sum(got, 0) / (Q * C)
        col_sums = column_sums(mean_grad)
        none = jnp.broadcast_to(col_sums[:Q], (Q, ROWS, COLS))
        return mean_grad, col_sums, none, none

    def exchange(x, groups):
        return lax.all_to_all(x, DP, 0, 0, axis_index_groups=groups, tiled=True)

    got = exchange(arrange(ahead, kept, other, weights), FIRST)
    sums = jnp.sum(got[:, : 4 * ROWS], 0).reshape(4, ROWS, COLS)
    rows = got[:, 4 * ROWS :].reshape(1, 4 * ahead, COLS)
    rows = jnp.broadcast_to(rows, (4, 4 * ahead, COLS))
    got = exchange(jnp.concatenate([sums, rows], 1), SECOND)
    mean_grad = jnp.sum(got[:, :ROWS], 0) / (Q * C)
    rows = got[:, ROWS:].reshape(Q, ahead, COLS)
    if ahead < ROWS:
        rows = jnp.pad(rows, ((0, 0), (0, ROWS - ahead), (0, 0)))
        others = jnp.zeros_like(rows)
    else:
        others = lax.ppermute(rows, "c", SWAP)
    return mean_grad, column_sums(mean_grad), rows, others


def back(ahead, scaled, parts, row, weights, own, others):
    if ahead:
        outs = back_early(ahead, scaled, parts, row, weights, own, others)
    else:
        outs = back_late(scaled, parts, row, weights)
    return outs[0].reshape(D, COLS), outs[1], outs[2].reshape(()), outs[3][0]


def back_early(ahead, scaled, parts, row, weights, own, others):
    if ahead < ROWS:
        own = own[:, :ahead]
        others = lax.ppermute(own, "c", SWAP)
    empty = jnp.zeros((6, COLS), jnp.float32)
    mine = share(jnp.concatenate([scaled, parts, empty, weights[ahead:]]), "q", Q)
    other = lax.ppermute(mine, "c", SWAP)
    return finish(ahead, mine, other, own, others, scaled, row)


def back_late(scaled, parts, row, weights):
    parts = share(parts, DP, Q * C)
    new, stepped, rms = step(parts, scaled, weights)
    mine = lax.all_to_all(stepped, "q", 0, 0, tiled=True)
    mine, new, rms, row = lax.optimization_barrier((mine, new, rms, row))
    other = lax.ppermute(mine, "c", SWAP)
    update, rms, row = small(new, rms, row)
    return lay(mine, other), update, rms, row


def per_device(replica_grads, weights, row_state, col_state):
    decay_rate = 1.0 - float(STEP) ** (-0.8)

    grads = replica_grads.reshape(Q, C, ROWS, COLS)
    core = lax.axis_index("c")
    sent = lax.dynamic_index_in_dim(grads, 1 - core, 1, False).astype(jnp.float32)
    sent, grads = lax.optimization_barrier((sent, grads))
    other = lax.ppermute(sent, "c", SWAP)
    kept = lax.dynamic_index_in_dim(grads, core, 1, False)
    kept = lax.optimization_barrier(kept.astype(jnp.float32))
    z = lax.axis_index("z")
    plane = jnp.where(z < 4, z // 2, jnp.minimum(z - 2, len(AHEAD) - 1))
    mean_grad, col_sums, own, others = lax.switch(
        plane, [functools.partial(front, n) for n in AHEAD], kept, other, weights
    )

    square = mean_grad * mean_grad + 1e-30
    col_sums = jnp.sum(col_sums, (0, 1))
    col_new = decay_rate * col_state + (1.0 - decay_rate) * (col_sums / D)
    both = jnp.stack(
        [jnp.sum(square, 1), jnp.sum(mean_grad * mean_grad * (1.0 / col_new), 1)]
    )
    both = jnp.sum(share(both, "z", Z), 0)
    row_new = decay_rate * row_state + (1.0 - decay_rate) * (both[0] / FLAT)
    scaled = mean_grad * lax.rsqrt(row_new[:, None] * col_new[None, :])
    parts = jnp.stack([row_new, both[1] / row_new])
    new_weights, update, rms_value, row_new = lax.switch(
        plane,
        [functools.partial(back, n) for n in AHEAD],
        *(scaled, parts, row_new[None], weights, own, others),
    )
    return (new_weights, update, row_new, col_new, rms_value)


def solution(mesh):
    split_mesh = Mesh(mesh.devices.reshape(Q, C, Z), ("q", "c", "z"))
    in_specs = (P(DP, None, "z"), P(DP, "z"), P(DP), P("z"))
    out_specs = (P(None, "z"), P(DP, "z"), P(DP), P("z"), P())
    return jax.shard_map(
        per_device,
        mesh=split_mesh,
        in_specs=in_specs,
        out_specs=out_specs,
        check_vma=False,
    )
```

```python
import functools

import jax
import jax.numpy as jnp
from jax import lax
from jax.experimental import pallas as pl
from jax.experimental.pallas import tpu as pltpu
from jax.sharding import Mesh, PartitionSpec as P

D = 4096
STEP = 10
FLAT = 2048
Q, C, Z = 16, 2, 16
ROWS = D // (Q * C)
COLS = FLAT // Z
AHEAD = (128, 112, 72, 48, 0)
SIDE = range(4)
ALONG_X = [[[(y * 4 + x) * C + c for x in SIDE] for y in SIDE] for c in range(C)]
ALONG_Y = [[[(y * 4 + x) * C + c for y in SIDE] for x in SIDE] for c in range(C)]
FIRST = ALONG_X[0] + ALONG_Y[1]
SECOND = ALONG_Y[0] + ALONG_X[1]
DP = ("q", "c")
SWAP = [(0, 1), (1, 0)]
VMEM = pl.BlockSpec(memory_space=pltpu.VMEM)
HBM = pl.BlockSpec(memory_space=pltpu.HBM)
ANY = pl.BlockSpec(memory_space=pl.ANY)


def share(x, axes, n):
    return lax.all_to_all(
        jnp.broadcast_to(x[None], (n, *x.shape)), axes, 0, 0, tiled=True
    )


def clip(ones, others):
    one, other = ones[0], others[0]
    for i in range(1, Q):
        one, other = one + ones[i], other + others[i]
    totals = jnp.sum(one + other, 1, keepdims=True)
    row_mean = totals[0:1] / D
    rms_value = jnp.sqrt(row_mean * totals[1:2] / (D * FLAT))
    return rms_value, jnp.sqrt(row_mean) / jnp.maximum(1.0, rms_value)


def step_body(parts, scaled, weights, update, stepped, rms):
    rms_value, gain = clip(
        [parts[C * i] for i in range(Q)], [parts[C * i + 1] for i in range(Q)]
    )
    new = scaled[...] * gain
    update[...] = new
    after = weights[...] - 0.001 * new
    for i in range(Q):
        stepped[i] = after
    rms[...] = rms_value


def step(parts, scaled, weights):
    return pl.pallas_call(
        step_body,
        out_shape=(
            jax.ShapeDtypeStruct((ROWS, COLS), jnp.float32),
            jax.ShapeDtypeStruct((Q, ROWS, COLS), jnp.float32),
            jax.ShapeDtypeStruct((1, 1), jnp.float32),
        ),
        in_specs=[VMEM, VMEM, VMEM],
        out_specs=(VMEM, VMEM, VMEM),
        compiler_params=pltpu.CompilerParams(vmem_limit_bytes=16 * 2**20),
        name="step",
    )(parts, scaled, weights)


def copy_all(pairs, sems):
    copies = [
        pltpu.make_async_copy(source, target, sems.at[i])
        for i, (source, target) in enumerate(pairs)
    ]
    for copy in copies:
        copy.start()
    for copy in copies:
        copy.wait()


def small_body(new, rms, row, update, rms_out, row_out, sems):
    copy_all([(new, update), (rms, rms_out), (row, row_out)], sems)


def small(new, rms, row):
    return pl.pallas_call(
        small_body,
        out_shape=(
            jax.ShapeDtypeStruct((ROWS, COLS), jnp.float32),
            jax.ShapeDtypeStruct((1, 1), jnp.float32),
            jax.ShapeDtypeStruct((1, ROWS), jnp.float32),
        ),
        in_specs=[ANY] * 3,
        out_specs=(HBM,) * 3,
        scratch_shapes=[pltpu.SemaphoreType.DMA((3,))],
        compiler_params=pltpu.CompilerParams(vmem_limit_bytes=16 * 2**20),
        cost_estimate=pl.CostEstimate(
            flops=0, bytes_accessed=Q * ROWS * COLS * 4, transcendentals=0
        ),
        name="small",
    )(new, rms, row)


def lay_body(mine, other, whole, sems):
    core = lax.axis_index("c")
    copy_all([(mine, whole.at[:, core]), (other, whole.at[:, 1 - core])], sems)


def lay(mine, other):
    return pl.pallas_call(
        lay_body,
        out_shape=jax.ShapeDtypeStruct((Q, C, ROWS, COLS), jnp.float32),
        in_specs=[ANY] * 2,
        out_specs=HBM,
        scratch_shapes=[pltpu.SemaphoreType.DMA((2,))],
        compiler_params=pltpu.CompilerParams(vmem_limit_bytes=16 * 2**20),
        name="lay",
    )(mine, other)


def finish_body(ahead, mine, other, own, others, scaled, row, *refs):
    whole, update, rms, row_out = refs
    core = lax.axis_index("c")
    tail = pl.ds(ROWS, 8)
    rms_value, gain = clip(
        [mine[i, tail][0:2] for i in range(Q)], [other[i, tail][0:2] for i in range(Q)]
    )
    rms[...] = rms_value
    update[...] = scaled[...] * gain
    row_out[...] = row[...]
    lowered = 0.001 * gain
    for j in range(Q):
        for side, rows, known in ((core, mine, own), (1 - core, other, others)):
            at = jnp.where(side == 0, j, j % 4 * 4 + j // 4)
            whole[j, side, :ahead] = known[at, :ahead] - lowered * rows[j, :ahead]
            if ahead < ROWS:
                whole[j, side, ahead:] = (
                    rows[j, ROWS + 8 :] - lowered * rows[j, ahead:ROWS]
                )


def finish(ahead, mine, other, own, others, scaled, row):
    whole = (Q, C, ROWS, COLS)
    return pl.pallas_call(
        functools.partial(finish_body, ahead),
        out_shape=(
            jax.ShapeDtypeStruct(whole, jnp.float32),
            jax.ShapeDtypeStruct((ROWS, COLS), jnp.float32),
            jax.ShapeDtypeStruct((1, 1), jnp.float32),
            jax.ShapeDtypeStruct((1, ROWS), jnp.float32),
        ),
        in_specs=[VMEM] * 6,
        out_specs=(VMEM,) * 4,
        compiler_params=pltpu.CompilerParams(vmem_limit_bytes=16 * 2**20),
        name="finish",
    )(mine, other, own, others, scaled, row)


def arrange_body(ahead, kept, other, weights, out):
    turn = lax.axis_index("c") == 0
    for i in range(4):
        for j in range(4):
            at = jnp.where(turn, j * 4 + i, i * 4 + j)
            out[i, j * ROWS : (j + 1) * ROWS] = kept[at] + other[at]
        out[i, 4 * ROWS :] = weights[:ahead]


def arrange(ahead, kept, other, weights):
    return pl.pallas_call(
        functools.partial(arrange_body, ahead),
        out_shape=jax.ShapeDtypeStruct((4, 4 * ROWS + ahead, COLS), jnp.float32),
        in_specs=[VMEM] * 3,
        out_specs=VMEM,
        compiler_params=pltpu.CompilerParams(vmem_limit_bytes=16 * 2**20),
        name="arrange",
    )(kept, other, weights)


def column_sums(mean_grad):
    square = mean_grad * mean_grad + 1e-30
    return share(jnp.sum(square, 0)[None], DP, Q * C)


def front(ahead, kept, other, weights):
    if not ahead:
        got = lax.all_to_all(kept + other, "q", 0, 0, tiled=True)
        mean_grad = jnp.sum(got, 0) / (Q * C)
        col_sums = column_sums(mean_grad)
        none = jnp.broadcast_to(col_sums[:Q], (Q, ROWS, COLS))
        return mean_grad, col_sums, none, none

    def exchange(x, groups):
        return lax.all_to_all(x, DP, 0, 0, axis_index_groups=groups, tiled=True)

    got = exchange(arrange(ahead, kept, other, weights), FIRST)
    sums = jnp.sum(got[:, : 4 * ROWS], 0).reshape(4, ROWS, COLS)
    rows = got[:, 4 * ROWS :].reshape(1, 4 * ahead, COLS)
    rows = jnp.broadcast_to(rows, (4, 4 * ahead, COLS))
    got = exchange(jnp.concatenate([sums, rows], 1), SECOND)
    mean_grad = jnp.sum(got[:, :ROWS], 0) / (Q * C)
    rows = got[:, ROWS:].reshape(Q, ahead, COLS)
    if ahead < ROWS:
        rows = jnp.pad(rows, ((0, 0), (0, ROWS - ahead), (0, 0)))
        others = jnp.zeros_like(rows)
    else:
        others = lax.ppermute(rows, "c", SWAP)
    return mean_grad, column_sums(mean_grad), rows, others


def back(ahead, scaled, parts, row, weights, own, others):
    if ahead:
        outs = back_early(ahead, scaled, parts, row, weights, own, others)
    else:
        outs = back_late(scaled, parts, row, weights)
    return outs[0].reshape(D, COLS), outs[1], outs[2].reshape(()), outs[3][0]


def back_early(ahead, scaled, parts, row, weights, own, others):
    if ahead < ROWS:
        own = own[:, :ahead]
        others = lax.ppermute(own, "c", SWAP)
    empty = jnp.zeros((6, COLS), jnp.float32)
    mine = share(jnp.concatenate([scaled, parts, empty, weights[ahead:]]), "q", Q)
    other = lax.ppermute(mine, "c", SWAP)
    return finish(ahead, mine, other, own, others, scaled, row)


def back_late(scaled, parts, row, weights):
    parts = share(parts, DP, Q * C)
    new, stepped, rms = step(parts, scaled, weights)
    mine = lax.all_to_all(stepped, "q", 0, 0, tiled=True)
    mine, new, rms, row = lax.optimization_barrier((mine, new, rms, row))
    other = lax.ppermute(mine, "c", SWAP)
    update, rms, row = small(new, rms, row)
    return lay(mine, other), update, rms, row


def per_device(replica_grads, weights, row_state, col_state):
    decay_rate = 1.0 - float(STEP) ** (-0.8)

    grads = replica_grads.reshape(Q, C, ROWS, COLS)
    core = lax.axis_index("c")
    sent = lax.dynamic_index_in_dim(grads, 1 - core, 1, False).astype(jnp.float32)
    sent, grads = lax.optimization_barrier((sent, grads))
    other = lax.ppermute(sent, "c", SWAP)
    kept = lax.dynamic_index_in_dim(grads, core, 1, False)
    kept = lax.optimization_barrier(kept.astype(jnp.float32))
    z = lax.axis_index("z")
    plane = jnp.where(z < 4, z // 2, jnp.minimum(z - 2, len(AHEAD) - 1))
    mean_grad, col_sums, own, others = lax.switch(
        plane, [functools.partial(front, n) for n in AHEAD], kept, other, weights
    )

    square = mean_grad * mean_grad + 1e-30
    col_sums = jnp.sum(col_sums, (0, 1))
    col_new = decay_rate * col_state + (1.0 - decay_rate) * (col_sums / D)
    both = jnp.stack(
        [jnp.sum(square, 1), jnp.sum(mean_grad * mean_grad * (1.0 / col_new), 1)]
    )
    both = jnp.sum(share(both, "z", Z), 0)
    row_new = decay_rate * row_state + (1.0 - decay_rate) * (both[0] / FLAT)
    scaled = mean_grad * lax.rsqrt(row_new[:, None] * col_new[None, :])
    parts = jnp.stack([row_new, both[1] / row_new])
    new_weights, update, rms_value, row_new = lax.switch(
        plane,
        [functools.partial(back, n) for n in AHEAD],
        *(scaled, parts, row_new[None], weights, own, others),
    )
    return (new_weights, update, row_new, col_new, rms_value)


def solution(mesh):
    split_mesh = Mesh(mesh.devices.reshape(Q, C, Z), ("q", "c", "z"))
    in_specs = (P(DP, None, "z"), P(DP, "z"), P(DP), P("z"))
    out_specs = (P(None, "z"), P(DP, "z"), P(DP), P("z"), P())
    return jax.shard_map(
        per_device,
        mesh=split_mesh,
        in_specs=in_specs,
        out_specs=out_specs,
        check_vma=False,
    )
```
